256 devices in a mesh: dp: 64 (over x_lo, y, z), rep: 4 (over x_hi, core).
Axes of the slice: x: 4 (x_hi: 2, x_lo: 2; x = x_hi * 2 + x_lo), y: 4, z: 8, core: 2. Of those that a mesh axis runs over, the one named last changes fastest.
Arguments:
- picture_embeds: bfloat16 [196608, 1152], P(('dp', 'rep')), may hold values from -0.1875 to 0.1875
- caption_embeds: bfloat16 [196608, 1152], P(('dp', 'rep')), may hold values from -0.1875 to 0.1875
- sharpness_multiplier: float32 [1], replicated, may hold values from 4 to 16
- offset_shift: float32 [1], replicated, may hold values from -4 to -1
Outputs:
- photo_entry_costs: float32 [196608], P(('dp', 'rep'))
- photo_adjoint: float32 [196608, 1152], P(('dp', 'rep'))
- sentence_adjoint: float32 [196608, 1152], P(('dp', 'rep'))
The draws below stay inside these ranges and needn't reach their ends.
All inputs are finite; a program needn't handle non-finite values.
Results may differ from the reference program's by a relative error of at most 0.0025.
Values may be sent and summed in bfloat16 or wider, within the bound.
A program may use at most 64 MiB of HBM per device.

```python
import math
import jax
import jax.numpy as jnp
from jax import lax

FEATURE_WIDTH = 1152
ROWS = 768
STEPS = 2
BATCH = 196608
N_DP = 64
N_REP = 4


def block_scale(rng, dims, split, smallest, largest):
    def one(axis_at, parts):
        heights = jax.random.uniform(jax.random.fold_in(jax.random.fold_in(rng, 6), axis_at), (parts,), jnp.float32, smallest / len(split), largest / len(split))
        return jnp.repeat(jnp.exp(heights), dims[axis_at] // parts).reshape((-1,) + (1,) * (len(dims) - axis_at - 1))

    gain = one(*split[0])
    for cut in split[1:]:
        gain = gain * one(*cut)
    return gain


def centred(stream_key, dims, scale, most, split=(), kind=jnp.bfloat16):
    result = jax.random.normal(stream_key, dims, jnp.float32) * scale
    if len(split) > 0:
        result = block_scale(stream_key, dims, split, -0.22, 0.18) * result
    return jnp.clip(result, min=-most, max=most).astype(kind)


def setup_inputs(seed: int = 0) -> dict:
    key_list = jax.random.split(jax.random.key(seed), 5)
    return {
        "picture_embeds": centred(key_list[0], (BATCH, FEATURE_WIDTH), FEATURE_WIDTH ** -0.5, 0.1875, ((0, 256),)),
        "caption_embeds": centred(key_list[1], (BATCH, FEATURE_WIDTH), FEATURE_WIDTH ** -0.5, 0.1875, ((0, 256),)),
        "sharpness_multiplier": jnp.clip(jnp.exp(jax.random.uniform(key_list[2], (1,), jnp.float32, math.log(4.0), math.log(16.0))), 4.0, 16.0),
        "offset_shift": jnp.clip(jax.random.uniform(key_list[3], (1,), jnp.float32, -4.0, -1.0), -4.0, -1.0),
    }


def matched_shares(picture_slab, caption_slab, sharpness_multiplier, offset_shift, resident_caption):
    similarity_table = sharpness_multiplier[0] * jnp.dot(picture_slab, caption_slab.T, preferred_element_type=jnp.float32) + offset_shift[0]
    if resident_caption:
        positive = jnp.eye(picture_slab.shape[0], dtype=jnp.float32)
    else:
        positive = jnp.zeros((picture_slab.shape[0], picture_slab.shape[0]), jnp.float32)
    sign = 2.0 * positive - 1.0
    loss = jnp.sum(-jax.nn.log_sigmoid(sign * similarity_table), axis=1)
    target_plus_minus = (jax.nn.sigmoid(similarity_table) - positive).astype(jnp.bfloat16)
    return loss, target_plus_minus


def reference(picture_embeds, caption_embeds, sharpness_multiplier, offset_shift):
    blocks = N_DP * N_REP
    img_blocks = picture_embeds.reshape(blocks, ROWS, FEATURE_WIDTH)
    txt_blocks = caption_embeds.reshape(blocks, ROWS, FEATURE_WIDTH)

    def photo_party(index):
        picture_slab = lax.dynamic_index_in_dim(img_blocks, index, 0, keepdims=False)
        loss = jnp.zeros((ROWS,), jnp.float32)
        odds_derivative = jnp.zeros((ROWS, FEATURE_WIDTH), jnp.float32)
        for circulation_round in range(STEPS + 1):
            other = ((index - circulation_round) % blocks).astype(jnp.int32)
            caption_slab = lax.dynamic_index_in_dim(txt_blocks, other, 0, keepdims=False)
            running_cost_total, target_plus_minus = matched_shares(picture_slab, caption_slab, sharpness_multiplier, offset_shift, circulation_round == 0)
            loss = loss + running_cost_total
            odds_derivative = odds_derivative + sharpness_multiplier[0] * jnp.dot(target_plus_minus, caption_slab, preferred_element_type=jnp.float32)
        return loss, odds_derivative

    def text_side(index):
        caption_slab = lax.dynamic_index_in_dim(txt_blocks, index, 0, keepdims=False)
        odds_derivative = jnp.zeros((ROWS, FEATURE_WIDTH), jnp.float32)
        for circulation_round in range(STEPS + 1):
            other = ((index + circulation_round) % blocks).astype(jnp.int32)
            picture_slab = lax.dynamic_index_in_dim(img_blocks, other, 0, keepdims=False)
            running_cost_total, target_plus_minus = matched_shares(picture_slab, caption_slab, sharpness_multiplier, offset_shift, circulation_round == 0)
            odds_derivative = odds_derivative + sharpness_multiplier[0] * jnp.dot(target_plus_minus.T, picture_slab, preferred_element_type=jnp.float32)
        return odds_derivative

    position_list = jnp.arange(blocks, dtype=jnp.int32)
    photo_entry_costs, photo_adjoint = lax.map(photo_party, position_list)
    sentence_adjoint = lax.map(text_side, position_list)
    return photo_entry_costs.reshape(-1), photo_adjoint.reshape(-1, FEATURE_WIDTH), sentence_adjoint.reshape(-1, FEATURE_WIDTH)
```

```python
import jax
import jax.numpy as jnp
from jax import lax
from jax.experimental import pallas as pl
from jax.experimental.pallas import tpu as pltpu
from jax.sharding import PartitionSpec as P

MESH = pl.DeviceIdType.MESH
N_REP = 4
DEVICES = 256
ROWS = 768
WIDTH = 1152
CHUNK = 128
CHUNKS = ROWS // CHUNK
TILE = 256
LATE_WINDOW = 3
EARLY_WINDOW = 2


def kernel(
    scale_ref, shift_ref, text_ref, image_ref,
    loss_out, image_out, text_out,
    own, got_far, got_near, beside, passed, grads, losses,
    load_sem, store_sem, far_send, far_recv, near_send, near_recv, pass_send, pass_recv, beside_sem,
):
    dp, rep = lax.axis_index("dp"), lax.axis_index("rep")
    parity = lax.rem(rep, 2)
    me = dp * N_REP + rep

    def place(index):
        index = lax.rem(index + DEVICES, DEVICES)
        return (index // N_REP, lax.rem(index, N_REP))

    far_target = place(me - 2 + 4 * parity)
    near_target = place(me + 2 - 4 * parity)
    partner = (dp, rep + 1 - 2 * parity)

    loads = [
        pltpu.make_async_copy(text_ref, own.at[parity], load_sem.at[0]),
        pltpu.make_async_copy(image_ref, own.at[1 - parity], load_sem.at[1]),
    ]
    for load in loads:
        load.start()
    barrier = pltpu.get_barrier_semaphore()
    for target in (far_target, near_target, partner):
        pl.semaphore_signal(barrier, inc=1, device_id=target, device_id_type=MESH)

    scale = scale_ref[0]
    shift = shift_ref[0]

    def rows(chunk):
        return pl.ds(pl.multiple_of(chunk * CHUNK, CHUNK), CHUNK)

    def far_copy(chunk):
        return pltpu.make_async_remote_copy(
            src_ref=own.at[1, rows(chunk)], dst_ref=got_far.at[rows(chunk)],
            send_sem=far_send.at[chunk], recv_sem=far_recv.at[chunk],
            device_id=far_target, device_id_type=MESH,
        )

    def near_copy(chunk):
        return pltpu.make_async_remote_copy(
            src_ref=own.at[0, rows(chunk)], dst_ref=got_near.at[rows(chunk)],
            send_sem=near_send.at[chunk], recv_sem=near_recv.at[chunk],
            device_id=near_target, device_id_type=MESH,
        )

    def pass_copy(chunk):
        return pltpu.make_async_remote_copy(
            src_ref=got_far.at[rows(chunk)], dst_ref=passed.at[rows(chunk)],
            send_sem=pass_send.at[chunk], recv_sem=pass_recv.at[chunk],
            device_id=partner, device_id_type=MESH,
        )

    beside_copy = pltpu.make_async_remote_copy(
        src_ref=own.at[0], dst_ref=beside, send_sem=beside_sem.at[0], recv_sem=beside_sem.at[1],
        device_id=partner, device_id_type=MESH,
    )

    def meet(slot, other, start, count, diagonal, finish=None):
        block = other[pl.ds(start, count), :]
        for tile in range(ROWS // TILE):
            part = pl.ds(tile * TILE, TILE)
            logits = (
                lax.dot_general(
                    own[slot, part, :], block, (((1,), (1,)), ((), ())), preferred_element_type=jnp.float32
                )
                * scale
                + shift
            )
            decay = jnp.exp(-jnp.abs(logits))
            chance = jnp.where(logits >= 0, 1.0, decay) / (1.0 + decay)
            if diagonal:
                row = lax.broadcasted_iota(jnp.int32, (TILE, count), 0) + tile * TILE
                column = lax.broadcasted_iota(jnp.int32, (TILE, count), 1) + start
                same = row == column
                coef = chance - jnp.where(same, 1.0, 0.0)
                against = jnp.where(same, -logits, logits)
            else:
                coef = chance
                against = logits
            cost = jnp.maximum(against, 0.0) + jnp.log1p(decay)
            total = cost[:, :128]
            for piece in range(1, count // 128):
                total = total + cost[:, piece * 128 : (piece + 1) * 128]
            losses[slot, part, :] += total
            change = jnp.dot(coef.astype(jnp.bfloat16), block, preferred_element_type=jnp.float32)
            if finish is None:
                grads[slot, part, :] += change
            else:
                grads[slot, part, :] = (grads[slot, part, :] + change) * scale
                finish(tile)

    grads[...] = jnp.zeros_like(grads)
    losses[...] = jnp.zeros_like(losses)
    for load in loads:
        load.wait()
    pl.semaphore_wait(barrier, 3)

    far_copy(0).start()
    near_copy(0).start()
    beside_copy.start()
    for chunk in range(1, LATE_WINDOW):
        far_copy(chunk).start()
        if chunk < EARLY_WINDOW:
            near_copy(chunk).start()

    def local(step, carry):
        start = pl.multiple_of(step * TILE, TILE)
        meet(0, own.at[1], start, TILE, True)
        meet(1, own.at[0], start, TILE, True)
        return carry

    lax.fori_loop(0, ROWS // TILE, local, 0)
    beside_copy.wait()

    def inside(step, carry):
        meet(0, beside, pl.multiple_of(step * TILE, TILE), TILE, False)
        return carry

    lax.fori_loop(0, ROWS // TILE, inside, 0)

    def take_far(chunk):
        copy = far_copy(chunk)
        copy.wait_recv()
        pass_copy(chunk).start()
        copy.wait_send()

        @pl.when(chunk + LATE_WINDOW < CHUNKS)
        def _():
            far_copy(chunk + LATE_WINDOW).start()

        meet(0, got_far, pl.multiple_of(chunk * CHUNK, CHUNK), CHUNK, False)

    def take_passed(chunk):
        pass_copy(chunk).wait()
        meet(1, passed, pl.multiple_of(chunk * CHUNK, CHUNK), CHUNK, False)

    def take_near(chunk):
        copy = near_copy(chunk)
        copy.wait_recv()
        copy.wait_send()

        @pl.when(chunk + EARLY_WINDOW < CHUNKS)
        def _():
            near_copy(chunk + EARLY_WINDOW).start()

        meet(1, got_near, pl.multiple_of(chunk * CHUNK, CHUNK), CHUNK, False)

    take_far(0)

    def across(chunk, carry):
        take_far(chunk)
        take_passed(chunk - 1)
        take_near(chunk - 1)
        return carry

    lax.fori_loop(1, CHUNKS, across, 0)

    grads[0] = grads[0] * scale

    def near_store(output):
        return pltpu.make_async_copy(grads.at[0], output, store_sem.at[ROWS // TILE])

    def far_store(output, tile):
        part = pl.ds(tile * TILE, TILE)
        return pltpu.make_async_copy(grads.at[1, part], output.at[part], store_sem.at[tile])

    @pl.when(parity == 0)
    def _():
        near_store(text_out).start()

    @pl.when(parity == 1)
    def _():
        near_store(image_out).start()

    take_passed(CHUNKS - 1)
    last = near_copy(CHUNKS - 1)
    last.wait_recv()
    last.wait_send()

    def finish(tile):
        @pl.when(parity == 0)
        def _():
            far_store(image_out, tile).start()

        @pl.when(parity == 1)
        def _():
            far_store(text_out, tile).start()

    meet(1, got_near, ROWS - CHUNK, CHUNK, False, finish)
    loss_out[...] = jnp.sum(losses[1 - parity].T, axis=0, keepdims=True)
    near_store(text_out).wait()
    for tile in range(ROWS // TILE):
        far_store(image_out, tile).wait()


def shards(picture_embeds, caption_embeds, sharpness_multiplier, offset_shift):
    smem = pl.BlockSpec(memory_space=pltpu.SMEM)
    hbm = pl.BlockSpec(memory_space=pl.ANY)
    block = pltpu.VMEM((ROWS, WIDTH), jnp.bfloat16)
    loss, image, text = pl.pallas_call(
        kernel,
        out_shape=[
            jax.ShapeDtypeStruct((1, ROWS), jnp.float32),
            jax.ShapeDtypeStruct((ROWS, WIDTH), jnp.float32),
            jax.ShapeDtypeStruct((ROWS, WIDTH), jnp.float32),
        ],
        in_specs=[smem, smem, hbm, hbm],
        out_specs=[pl.BlockSpec(memory_space=pltpu.VMEM), hbm, hbm],
        scratch_shapes=[
            pltpu.VMEM((2, ROWS, WIDTH), jnp.bfloat16),
            block, block, block, block,
            pltpu.VMEM((2, ROWS, WIDTH), jnp.float32),
            pltpu.VMEM((2, ROWS, 128), jnp.float32),
            pltpu.SemaphoreType.DMA((2,)),
            pltpu.SemaphoreType.DMA((ROWS // TILE + 1,)),
            pltpu.SemaphoreType.DMA((CHUNKS,)),
            pltpu.SemaphoreType.DMA((CHUNKS,)),
            pltpu.SemaphoreType.DMA((CHUNKS,)),
            pltpu.SemaphoreType.DMA((CHUNKS,)),
            pltpu.SemaphoreType.DMA((CHUNKS,)),
            pltpu.SemaphoreType.DMA((CHUNKS,)),
            pltpu.SemaphoreType.DMA((2,)),
        ],
        compiler_params=pltpu.CompilerParams(
            collective_id=0, has_side_effects=True, vmem_limit_bytes=48 * 2**20
        ),
        cost_estimate=pl.CostEstimate(
            flops=24 * ROWS * ROWS * WIDTH, bytes_accessed=12 * ROWS * WIDTH, transcendentals=18 * ROWS * ROWS
        ),
    )(sharpness_multiplier, offset_shift, caption_embeds, picture_embeds)
    return loss.reshape(ROWS), image, text


def solution(mesh):
    in_specs = (P(("dp", "rep"), None), P(("dp", "rep"), None), P(), P())
    out_specs = (P(("dp", "rep")), P(("dp", "rep"), None), P(("dp", "rep"), None))
    return jax.shard_map(shards, mesh=mesh, in_specs=in_specs, out_specs=out_specs, check_vma=False)
```

```python
import jax
import jax.numpy as jnp
from jax import lax
from jax.experimental import pallas as pl
from jax.experimental.pallas import tpu as pltpu
from jax.sharding import PartitionSpec as P

MESH = pl.DeviceIdType.MESH
N_REP = 4
DEVICES = 256
ROWS = 768
WIDTH = 1152
CHUNK = 128
CHUNKS = ROWS // CHUNK
TILE = 256
FAR_WINDOW = 3
NEAR_WINDOW = 2


def meet(near_or_far, block, scale, shift, tile, start=None):
    part = pl.ds(pl.multiple_of(jnp.int32(tile) * TILE, TILE), TILE)
    count = block.shape[0]
    logits = (
        lax.dot_general(
            near_or_far[part, :], block, (((1,), (1,)), ((), ())), preferred_element_type=jnp.float32
        )
        * scale
        + shift
    )
    decay = jnp.exp(-jnp.abs(logits))
    chance = jnp.where(logits >= 0, 1.0, decay) / (1.0 + decay)
    if start is not None:
        row = lax.broadcasted_iota(jnp.int32, (TILE, count), 0) + tile * TILE
        column = lax.broadcasted_iota(jnp.int32, (TILE, count), 1) + start
        same = row == column
        chance = chance - jnp.where(same, 1.0, 0.0)
        logits = jnp.where(same, -logits, logits)
    cost = jnp.maximum(logits, 0.0) + jnp.log1p(decay)
    total = cost[:, :128]
    for piece in range(1, count // 128):
        total = total + cost[:, piece * 128 : (piece + 1) * 128]
    change = jnp.dot(chance.astype(jnp.bfloat16), block, preferred_element_type=jnp.float32)
    return total, change


def kernel(
    scale_ref, shift_ref, text_ref, image_ref,
    own, got_near, grads, losses,
    got_far, beside, passed,
    load_sem, far_send, far_recv, near_send, near_recv, pass_send, pass_recv, beside_sem,
):
    dp, rep = lax.axis_index("dp"), lax.axis_index("rep")
    parity = lax.rem(rep, 2)
    me = dp * N_REP + rep

    def place(index):
        index = lax.rem(index + DEVICES, DEVICES)
        return (index // N_REP, lax.rem(index, N_REP))

    far_target = place(me - 2 + 4 * parity)
    near_target = place(me + 2 - 4 * parity)
    partner = (dp, rep + 1 - 2 * parity)

    loads = [
        pltpu.make_async_copy(text_ref, own.at[parity], load_sem.at[0]),
        pltpu.make_async_copy(image_ref, own.at[1 - parity], load_sem.at[1]),
    ]
    for load in loads:
        load.start()
    barrier = pltpu.get_barrier_semaphore()
    for target in (far_target, near_target, partner):
        pl.semaphore_signal(barrier, inc=1, device_id=target, device_id_type=MESH)

    scale = scale_ref[0]
    shift = shift_ref[0]

    def rows(chunk):
        return pl.ds(pl.multiple_of(chunk * CHUNK, CHUNK), CHUNK)

    def far_copy(chunk, source=image_ref):
        return pltpu.make_async_remote_copy(
            src_ref=source.at[rows(chunk)], dst_ref=got_far.at[rows(chunk)],
            send_sem=far_send.at[chunk], recv_sem=far_recv.at[chunk],
            device_id=far_target, device_id_type=MESH,
        )

    def near_copy(chunk, source=text_ref):
        return pltpu.make_async_remote_copy(
            src_ref=source.at[rows(chunk)], dst_ref=got_near.at[rows(chunk)],
            send_sem=near_send.at[chunk], recv_sem=near_recv.at[chunk],
            device_id=near_target, device_id_type=MESH,
        )

    def beside_copy(source=text_ref):
        return pltpu.make_async_remote_copy(
            src_ref=source, dst_ref=beside, send_sem=beside_sem.at[0], recv_sem=beside_sem.at[1],
            device_id=partner, device_id_type=MESH,
        )

    def pass_copy(chunk):
        return pltpu.make_async_remote_copy(
            src_ref=got_far.at[rows(chunk)], dst_ref=passed.at[rows(chunk)],
            send_sem=pass_send.at[chunk], recv_sem=pass_recv.at[chunk],
            device_id=partner, device_id_type=MESH,
        )

    def send(fars, nears, with_beside=False):
        for side, (far_source, near_source) in enumerate(((image_ref, text_ref), (text_ref, image_ref))):

            @pl.when(parity == side)
            def _():
                for step in range(max(len(fars), len(nears))):
                    if step < len(fars):
                        far_copy(fars[step], far_source).start()
                    if step < len(nears):
                        near_copy(nears[step], near_source).start()
                    if step == 0 and with_beside:
                        beside_copy(near_source).start()

    def gather(slot, other, start, count, diagonal=False, factor=None):
        block = other[pl.ds(start, count), :]

        def one(tile, carry):
            part = pl.ds(pl.multiple_of(tile * TILE, TILE), TILE)
            total, change = meet(own.at[slot], block, scale, shift, tile, start if diagonal else None)
            losses[slot, part, :] += total
            if factor is None:
                grads[slot, part, :] += change
            else:
                grads[slot, part, :] = (grads[slot, part, :] + change) * factor
            return carry

        lax.fori_loop(0, ROWS // TILE, one, 0)

    pl.semaphore_wait(barrier, 3)
    send(range(FAR_WINDOW), range(NEAR_WINDOW), True)
    grads[...] = jnp.zeros_like(grads)
    losses[...] = jnp.zeros_like(losses)
    for load in loads:
        load.wait()

    def local(step, carry):
        start = pl.multiple_of(step * TILE, TILE)
        gather(0, own.at[1], start, TILE, True)
        gather(1, own.at[0], start, TILE, True)
        return carry

    lax.fori_loop(0, ROWS // TILE, local, 0)
    beside_copy().wait()

    def inside(step, carry):
        gather(0, beside, pl.multiple_of(step * TILE, TILE), TILE)
        return carry

    lax.fori_loop(0, ROWS // TILE, inside, 0)

    def take_far(chunk):
        copy = far_copy(chunk)
        copy.wait_recv()
        pass_copy(chunk).start()
        copy.wait_send()

        @pl.when(chunk + FAR_WINDOW < CHUNKS)
        def _():
            send([chunk + FAR_WINDOW], [])

        factor = jnp.where(chunk == CHUNKS - 1, scale, 1.0)
        gather(0, got_far, pl.multiple_of(chunk * CHUNK, CHUNK), CHUNK, False, factor)

    def take_passed(chunk):
        pass_copy(chunk).wait()
        gather(1, passed, pl.multiple_of(chunk * CHUNK, CHUNK), CHUNK)

    def take_near(chunk):
        copy = near_copy(chunk)
        copy.wait_recv()
        copy.wait_send()

        @pl.when(chunk + NEAR_WINDOW < CHUNKS)
        def _():
            send([], [chunk + NEAR_WINDOW])

        @pl.when(chunk < CHUNKS - 1)
        def _():
            gather(1, got_near, pl.multiple_of(chunk * CHUNK, CHUNK), CHUNK)

    def across(chunk, carry):
        @pl.when(chunk >= 1)
        def _():
            take_passed(chunk - 1)

        @pl.when(chunk < CHUNKS)
        def _():
            take_far(chunk)

        @pl.when(chunk >= 1)
        def _():
            take_near(chunk - 1)

        return carry

    lax.fori_loop(0, CHUNKS + 1, across, 0)


def closing(scale_ref, shift_ref, own, got_near, grads, losses, loss_out, image_out, text_out, scaled, cost, sem):
    parity = lax.rem(lax.axis_index("rep"), 2)
    scale = scale_ref[0]
    shift = shift_ref[0]
    tiles = ROWS // TILE

    def store(source, output, tile, which):
        part = pl.ds(tile * TILE, TILE)
        return pltpu.make_async_copy(source.at[part], output.at[part], sem.at[which * tiles + tile])

    for side, output in enumerate((text_out, image_out)):

        @pl.when(parity == side)
        def _():
            for tile in range(tiles):
                store(grads.at[0], output, tile, 0).start()

    block = got_near[pl.ds(ROWS - CHUNK, CHUNK), :]
    for tile in range(tiles):
        part = pl.ds(tile * TILE, TILE)
        total, change = meet(own.at[1], block, scale, shift, tile)
        scaled[part, :] = (grads[1, part, :] + change) * scale

        for side, output in enumerate((image_out, text_out)):

            @pl.when(parity == side)
            def _():
                store(scaled, output, tile, 1).start()

        image_losses = jnp.where(parity == 0, losses[1, part, :] + total, losses[0, part, :])
        cost[part] = jnp.sum(image_losses.T, axis=0)
    loss_store = pltpu.make_async_copy(cost, loss_out, sem.at[2 * tiles])
    loss_store.start()
    for tile in range(tiles):
        store(grads.at[0], text_out, tile, 0).wait()
        store(scaled, image_out, tile, 1).wait()
    loss_store.wait()


def shards(picture_embeds, caption_embeds, sharpness_multiplier, offset_shift):
    smem = pl.BlockSpec(memory_space=pltpu.SMEM)
    vmem = pl.BlockSpec(memory_space=pltpu.VMEM)
    hbm = pl.BlockSpec(memory_space=pltpu.HBM)
    block = pltpu.VMEM((ROWS, WIDTH), jnp.bfloat16)
    chunk_sems = pltpu.SemaphoreType.DMA((CHUNKS,))
    kept = pl.pallas_call(
        kernel,
        out_shape=[
            pltpu.VMEM((2, ROWS, WIDTH), jnp.bfloat16),
            pltpu.VMEM((ROWS, WIDTH), jnp.bfloat16),
            pltpu.VMEM((2, ROWS, WIDTH), jnp.float32),
            pltpu.VMEM((2, ROWS, 128), jnp.float32),
        ],
        in_specs=[smem, smem, hbm, hbm],
        out_specs=[vmem] * 4,
        scratch_shapes=[
            block, block, block,
            pltpu.SemaphoreType.DMA((2,)),
            chunk_sems, chunk_sems, chunk_sems, chunk_sems, chunk_sems, chunk_sems,
            pltpu.SemaphoreType.DMA((2,)),
        ],
        compiler_params=pltpu.CompilerParams(
            collective_id=0, has_side_effects=True, vmem_limit_bytes=40 * 2**20
        ),
        cost_estimate=pl.CostEstimate(
            flops=24 * ROWS * ROWS * WIDTH, bytes_accessed=12 * ROWS * WIDTH, transcendentals=18 * ROWS * ROWS
        ),
    )(
        sharpness_multiplier,
        offset_shift,
        pltpu.with_memory_space_constraint(caption_embeds, pltpu.HBM),
        pltpu.with_memory_space_constraint(picture_embeds, pltpu.HBM),
    )
    kept = [pltpu.with_memory_space_constraint(value, pltpu.VMEM) for value in kept]
    return pl.pallas_call(
        closing,
        out_shape=[
            jax.ShapeDtypeStruct((ROWS,), jnp.float32),
            jax.ShapeDtypeStruct((ROWS, WIDTH), jnp.float32),
            jax.ShapeDtypeStruct((ROWS, WIDTH), jnp.float32),
        ],
        in_specs=[smem, smem, vmem, vmem, vmem, vmem],
        out_specs=[hbm, hbm, hbm],
        scratch_shapes=[
            pltpu.VMEM((ROWS, WIDTH), jnp.float32),
            pltpu.VMEM((ROWS,), jnp.float32),
            pltpu.SemaphoreType.DMA((2 * ROWS // TILE + 1,)),
        ],
        compiler_params=pltpu.CompilerParams(vmem_limit_bytes=40 * 2**20),
        cost_estimate=pl.CostEstimate(
            flops=4 * CHUNK * ROWS * WIDTH, bytes_accessed=8 * ROWS * WIDTH, transcendentals=3 * CHUNK * ROWS
        ),
    )(sharpness_multiplier, offset_shift, *kept)


def solution(mesh):
    in_specs = (P(("dp", "rep"), None), P(("dp", "rep"), None), P(), P())
    out_specs = (P(("dp", "rep")), P(("dp", "rep"), None), P(("dp", "rep"), None))
    return jax.shard_map(shards, mesh=mesh, in_specs=in_specs, out_specs=out_specs, check_vma=False)
```

```python
import jax
import jax.numpy as jnp
from jax import lax
from jax.experimental import pallas as pl
from jax.experimental.pallas import tpu as pltpu
from jax.sharding import PartitionSpec as P

MESH = pl.DeviceIdType.MESH
N_REP = 4
DEVICES = 256
ROWS = 768
WIDTH = 1152
CHUNK = 128
CHUNKS = ROWS // CHUNK
TILE = 256
WINDOW = 2


def meet(near_or_far, block, scale, shift, tile, start=None):
    part = pl.ds(pl.multiple_of(jnp.int32(tile) * TILE, TILE), TILE)
    count = block.shape[0]
    logits = (
        lax.dot_general(
            near_or_far[part, :], block, (((1,), (1,)), ((), ())), preferred_element_type=jnp.float32
        )
        * scale
        + shift
    )
    decay = jnp.exp(-jnp.abs(logits))
    above = 1.0 + decay
    inverse = pl.reciprocal(above, approx=True)
    inverse = inverse * (2.0 - above * inverse)
    chance = jnp.where(logits >= 0, inverse, decay * inverse)
    log_above = jnp.log(above) + (decay - (above - 1.0)) * inverse
    if start is not None:
        row = lax.broadcasted_iota(jnp.int32, (TILE, count), 0) + tile * TILE
        column = lax.broadcasted_iota(jnp.int32, (TILE, count), 1) + start
        same = row == column
        chance = chance - jnp.where(same, 1.0, 0.0)
        logits = jnp.where(same, -logits, logits)
    cost = jnp.maximum(logits, 0.0) + log_above
    total = cost[:, : min(count, 128)]
    for piece in range(1, count // 128):
        total = total + cost[:, piece * 128 : (piece + 1) * 128]
    change = jnp.dot(chance.astype(jnp.bfloat16), block, preferred_element_type=jnp.float32)
    return total, change


def kernel(
    scale_ref, shift_ref, text_ref, image_ref,
    own, got_near, grads, losses,
    got_far, beside, passed,
    load_sem, far_send, far_recv, near_send, near_recv, pass_send, pass_recv, beside_sem,
):
    dp, rep = lax.axis_index("dp"), lax.axis_index("rep")
    parity = lax.rem(rep, 2)
    me = dp * N_REP + rep

    def place(index):
        index = lax.rem(index + DEVICES, DEVICES)
        return (index // N_REP, lax.rem(index, N_REP))

    far_target = place(me - 2 + 4 * parity)
    near_target = place(me + 2 - 4 * parity)
    partner = (dp, rep + 1 - 2 * parity)

    loads = [
        pltpu.make_async_copy(text_ref, own.at[parity], load_sem.at[0]),
        pltpu.make_async_copy(image_ref, own.at[1 - parity], load_sem.at[1]),
    ]
    for load in loads:
        load.start()
    barrier = pltpu.get_barrier_semaphore()
    for target in (far_target, near_target, partner):
        pl.semaphore_signal(barrier, inc=1, device_id=target, device_id_type=MESH)

    scale = scale_ref[0]
    shift = shift_ref[0]

    def rows(chunk):
        return pl.ds(pl.multiple_of(chunk * CHUNK, CHUNK), CHUNK)

    def far_copy(chunk, source=image_ref):
        return pltpu.make_async_remote_copy(
            src_ref=source.at[rows(chunk)], dst_ref=got_far.at[rows(chunk)],
            send_sem=far_send.at[chunk], recv_sem=far_recv.at[chunk],
            device_id=far_target, device_id_type=MESH,
        )

    def near_copy(chunk, source=text_ref):
        return pltpu.make_async_remote_copy(
            src_ref=source.at[rows(chunk)], dst_ref=got_near.at[rows(chunk)],
            send_sem=near_send.at[chunk], recv_sem=near_recv.at[chunk],
            device_id=near_target, device_id_type=MESH,
        )

    def beside_copy(source=text_ref):
        return pltpu.make_async_remote_copy(
            src_ref=source, dst_ref=beside, send_sem=beside_sem.at[0], recv_sem=beside_sem.at[1],
            device_id=partner, device_id_type=MESH,
        )

    def pass_copy(chunk):
        return pltpu.make_async_remote_copy(
            src_ref=got_far.at[rows(chunk)], dst_ref=passed.at[rows(chunk)],
            send_sem=pass_send.at[chunk], recv_sem=pass_recv.at[chunk],
            device_id=partner, device_id_type=MESH,
        )

    def send(fars, nears, with_beside=False):
        for side, (far_source, near_source) in enumerate(((image_ref, text_ref), (text_ref, image_ref))):

            @pl.when(parity == side)
            def _():
                for step in range(max(len(fars), len(nears))):
                    if step < len(fars):
                        far_copy(fars[step], far_source).start()
                    if step < len(nears):
                        near_copy(nears[step], near_source).start()
                    if step == 0 and with_beside:
                        beside_copy(near_source).start()

    def gather(slot, other, start, count, diagonal=False, factor=None):
        block = other[pl.ds(start, count), :]

        def one(tile, carry):
            part = pl.ds(pl.multiple_of(tile * TILE, TILE), TILE)
            total, change = meet(own.at[slot], block, scale, shift, tile, start if diagonal else None)
            losses[slot, part, : total.shape[1]] += total
            if factor is None:
                grads[slot, part, :] += change
            else:
                grads[slot, part, :] = (grads[slot, part, :] + change) * factor
            return carry

        for tile in range(ROWS // TILE):
            one(tile, 0)

    pl.semaphore_wait(barrier, 3)
    send(range(WINDOW), [], True)
    grads[...] = jnp.zeros_like(grads)
    losses[...] = jnp.zeros_like(losses)
    for load in loads:
        load.wait()
    send([], range(WINDOW))

    def local(step, carry):
        slot = lax.rem(step, 2)
        gather(slot, own.at[1 - slot], pl.multiple_of(step // 2 * TILE, TILE), TILE, True)
        return carry

    lax.fori_loop(0, 2 * ROWS // TILE, local, 0)
    beside_copy().wait()

    def inside(step, carry):
        gather(0, beside, pl.multiple_of(step * TILE, TILE), 256)
        return carry

    lax.fori_loop(0, ROWS // TILE, inside, 0)

    def refill_far(chunk):
        far_copy(chunk).wait_send()

        @pl.when(chunk + WINDOW < CHUNKS)
        def _():
            send([chunk + WINDOW], [])

    def refill_near(chunk):
        near_copy(chunk).wait_send()

        @pl.when(chunk + WINDOW < CHUNKS)
        def _():
            send([], [chunk + WINDOW])

    def across(chunk, carry):
        start = pl.multiple_of(chunk * CHUNK, CHUNK)
        refill_far(chunk)
        far_copy(chunk).wait_recv()
        pass_copy(chunk).start()
        gather(0, got_far, start, CHUNK, False, jnp.where(chunk == CHUNKS - 1, scale, 1.0))
        pass_copy(chunk).wait()
        gather(1, passed, start, CHUNK)
        refill_near(chunk)
        near_copy(chunk).wait_recv()

        @pl.when(chunk < CHUNKS - 1)
        def _():
            gather(1, got_near, start, CHUNK)

        return carry

    lax.fori_loop(0, CHUNKS, across, 0)


def closing(scale_ref, shift_ref, own, got_near, grads, losses, loss_out, image_out, text_out, scaled, cost, sem):
    parity = lax.rem(lax.axis_index("rep"), 2)
    scale = scale_ref[0]
    shift = shift_ref[0]
    tiles = ROWS // TILE

    def store(source, output, tile, which):
        part = pl.ds(tile * TILE, TILE)
        return pltpu.make_async_copy(source.at[part], output.at[part], sem.at[which * tiles + tile])

    for side, output in enumerate((text_out, image_out)):

        @pl.when(parity == side)
        def _():
            for tile in range(tiles):
                store(grads.at[0], output, tile, 0).start()

    block = got_near[pl.ds(ROWS - CHUNK, CHUNK), :]
    for tile in range(tiles):
        part = pl.ds(tile * TILE, TILE)
        total, change = meet(own.at[1], block, scale, shift, tile)
        scaled[part, :] = (grads[1, part, :] + change) * scale

        for side, output in enumerate((image_out, text_out)):

            @pl.when(parity == side)
            def _():
                store(scaled, output, tile, 1).start()

        image_losses = jnp.where(parity == 0, losses[1, part, :] + total, losses[0, part, :])
        cost[part] = jnp.sum(image_losses.T, axis=0)
    loss_store = pltpu.make_async_copy(cost, loss_out, sem.at[2 * tiles])
    loss_store.start()
    for tile in range(tiles):
        store(grads.at[0], text_out, tile, 0).wait()
        store(scaled, image_out, tile, 1).wait()
    loss_store.wait()


def shards(picture_embeds, caption_embeds, sharpness_multiplier, offset_shift):
    smem = pl.BlockSpec(memory_space=pltpu.SMEM)
    vmem = pl.BlockSpec(memory_space=pltpu.VMEM)
    hbm = pl.BlockSpec(memory_space=pltpu.HBM)
    block = pltpu.VMEM((ROWS, WIDTH), jnp.bfloat16)
    chunk_sems = pltpu.SemaphoreType.DMA((CHUNKS,))
    kept = pl.pallas_call(
        kernel,
        out_shape=[
            pltpu.VMEM((2, ROWS, WIDTH), jnp.bfloat16),
            pltpu.VMEM((ROWS, WIDTH), jnp.bfloat16),
            pltpu.VMEM((2, ROWS, WIDTH), jnp.float32),
            pltpu.VMEM((2, ROWS, 128), jnp.float32),
        ],
        in_specs=[smem, smem, hbm, hbm],
        out_specs=[vmem] * 4,
        scratch_shapes=[
            block, block, block,
            pltpu.SemaphoreType.DMA((2,)),
            chunk_sems, chunk_sems, chunk_sems, chunk_sems, chunk_sems, chunk_sems,
            pltpu.SemaphoreType.DMA((2,)),
        ],
        compiler_params=pltpu.CompilerParams(
            collective_id=0, has_side_effects=True, vmem_limit_bytes=40 * 2**20
        ),
        cost_estimate=pl.CostEstimate(
            flops=24 * ROWS * ROWS * WIDTH, bytes_accessed=12 * ROWS * WIDTH, transcendentals=18 * ROWS * ROWS
        ),
    )(
        sharpness_multiplier,
        offset_shift,
        pltpu.with_memory_space_constraint(caption_embeds, pltpu.HBM),
        pltpu.with_memory_space_constraint(picture_embeds, pltpu.HBM),
    )
    kept = [pltpu.with_memory_space_constraint(value, pltpu.VMEM) for value in kept]
    return pl.pallas_call(
        closing,
        out_shape=[
            jax.ShapeDtypeStruct((ROWS,), jnp.float32),
            jax.ShapeDtypeStruct((ROWS, WIDTH), jnp.float32),
            jax.ShapeDtypeStruct((ROWS, WIDTH), jnp.float32),
        ],
        in_specs=[smem, smem, vmem, vmem, vmem, vmem],
        out_specs=[hbm, hbm, hbm],
        scratch_shapes=[
            pltpu.VMEM((ROWS, WIDTH), jnp.float32),
            pltpu.VMEM((ROWS,), jnp.float32),
            pltpu.SemaphoreType.DMA((2 * ROWS // TILE + 1,)),
        ],
        compiler_params=pltpu.CompilerParams(vmem_limit_bytes=40 * 2**20),
        cost_estimate=pl.CostEstimate(
            flops=4 * CHUNK * ROWS * WIDTH, bytes_accessed=8 * ROWS * WIDTH, transcendentals=3 * CHUNK * ROWS
        ),
    )(sharpness_multiplier, offset_shift, *kept)


def solution(mesh):
    in_specs = (P(("dp", "rep"), None), P(("dp", "rep"), None), P(), P())
    out_specs = (P(("dp", "rep")), P(("dp", "rep"), None), P(("dp", "rep"), None))
    return jax.shard_map(shards, mesh=mesh, in_specs=in_specs, out_specs=out_specs, check_vma=False)
```

```python
import jax
import jax.numpy as jnp
from jax import lax
from jax.experimental import pallas as pl
from jax.experimental.pallas import tpu as pltpu
from jax.sharding import PartitionSpec as P

MESH = pl.DeviceIdType.MESH
N_REP = 4
DEVICES = 256
ROWS = 768
WIDTH = 1152
CHUNK = 128
CHUNKS = ROWS // CHUNK
TILE = 256
WINDOW = 2


def meet(near_or_far, block, scale, shift, tile, start=None):
    part = pl.ds(pl.multiple_of(jnp.int32(tile) * TILE, TILE), TILE)
    count = block.shape[0]
    logits = (
        lax.dot_general(
            near_or_far[part, :], block, (((1,), (1,)), ((), ())), preferred_element_type=jnp.float32
        )
        * scale
        + shift
    )
    decay = jnp.exp(-jnp.abs(logits))
    above = 1.0 + decay
    inverse = pl.reciprocal(above, approx=True)
    inverse = inverse * (2.0 - above * inverse)
    chance = jnp.where(logits >= 0, inverse, decay * inverse)
    log_above = jnp.log(above) + (decay - (above - 1.0)) * inverse
    if start is not None:
        row = lax.broadcasted_iota(jnp.int32, (TILE, count), 0) + tile * TILE
        column = lax.broadcasted_iota(jnp.int32, (TILE, count), 1) + start
        same = row == column
        chance = chance - jnp.where(same, 1.0, 0.0)
        logits = jnp.where(same, -logits, logits)
    cost = jnp.maximum(logits, 0.0) + log_above
    total = cost[:, : min(count, 128)]
    for piece in range(1, count // 128):
        total = total + cost[:, piece * 128 : (piece + 1) * 128]
    change = jnp.dot(chance.astype(jnp.bfloat16), block, preferred_element_type=jnp.float32)
    return total, change


def kernel(
    scale_ref, shift_ref, text_ref, image_ref,
    own, met, grads, losses,
    got_far, beside,
    load_sem, far_send, far_recv, near_send, near_recv, pass_send, pass_recv, beside_sem,
):
    dp, rep = lax.axis_index("dp"), lax.axis_index("rep")
    parity = lax.rem(rep, 2)
    me = dp * N_REP + rep

    def place(index):
        index = lax.rem(index + DEVICES, DEVICES)
        return (index // N_REP, lax.rem(index, N_REP))

    far_target = place(me - 2 + 4 * parity)
    near_target = place(me + 2 - 4 * parity)
    partner = (dp, rep + 1 - 2 * parity)

    loads = [
        pltpu.make_async_copy(text_ref, own.at[parity], load_sem.at[0]),
        pltpu.make_async_copy(image_ref, own.at[1 - parity], load_sem.at[1]),
    ]
    for load in loads:
        load.start()
    barrier = pltpu.get_barrier_semaphore()
    for target in (far_target, near_target, partner):
        pl.semaphore_signal(barrier, inc=1, device_id=target, device_id_type=MESH)

    scale = scale_ref[0]
    shift = shift_ref[0]

    def rows(chunk):
        return pl.ds(pl.multiple_of(chunk * CHUNK, CHUNK), CHUNK)

    def far_copy(chunk, source=image_ref):
        return pltpu.make_async_remote_copy(
            src_ref=source.at[rows(chunk)], dst_ref=got_far.at[rows(chunk)],
            send_sem=far_send.at[chunk], recv_sem=far_recv.at[chunk],
            device_id=far_target, device_id_type=MESH,
        )

    def near_copy(chunk, source=text_ref):
        return pltpu.make_async_remote_copy(
            src_ref=source.at[rows(chunk)], dst_ref=met.at[rows(2 * chunk + 1)],
            send_sem=near_send.at[chunk], recv_sem=near_recv.at[chunk],
            device_id=near_target, device_id_type=MESH,
        )

    def beside_copy(source=text_ref):
        return pltpu.make_async_remote_copy(
            src_ref=source, dst_ref=beside, send_sem=beside_sem.at[0], recv_sem=beside_sem.at[1],
            device_id=partner, device_id_type=MESH,
        )

    def pass_copy(chunk):
        return pltpu.make_async_remote_copy(
            src_ref=got_far.at[rows(chunk)], dst_ref=met.at[rows(2 * chunk)],
            send_sem=pass_send.at[chunk], recv_sem=pass_recv.at[chunk],
            device_id=partner, device_id_type=MESH,
        )

    def send(fars, nears, with_beside=False):
        for side, (far_source, near_source) in enumerate(((image_ref, text_ref), (text_ref, image_ref))):

            @pl.when(parity == side)
            def _():
                for step in range(max(len(fars), len(nears))):
                    if step < len(fars):
                        far_copy(fars[step], far_source).start()
                    if step < len(nears):
                        near_copy(nears[step], near_source).start()
                    if step == 0 and with_beside:
                        beside_copy(near_source).start()

    def gather(slot, other, start, count, diagonal=False, factor=None):
        block = other[pl.ds(start, count), :]

        def one(tile, carry):
            part = pl.ds(pl.multiple_of(tile * TILE, TILE), TILE)
            total, change = meet(own.at[slot], block, scale, shift, tile, start if diagonal else None)
            losses[slot, part, : total.shape[1]] += total
            if factor is None:
                grads[slot, part, :] += change
            else:
                grads[slot, part, :] = (grads[slot, part, :] + change) * factor
            return carry

        for tile in range(ROWS // TILE):
            one(tile, 0)

    pl.semaphore_wait(barrier, 3)
    send(range(WINDOW), [], True)
    grads[...] = jnp.zeros_like(grads)
    losses[...] = jnp.zeros_like(losses)
    for load in loads:
        load.wait()
    send([], range(WINDOW))

    def local(step, carry):
        slot = lax.rem(step, 2)
        gather(slot, own.at[1 - slot], pl.multiple_of(step // 2 * TILE, TILE), TILE, True)
        return carry

    lax.fori_loop(0, 2 * ROWS // TILE, local, 0)
    beside_copy().wait()

    def inside(step, carry):
        gather(0, beside, pl.multiple_of(step * TILE, TILE), 256)
        return carry

    lax.fori_loop(0, ROWS // TILE, inside, 0)

    def refill_far(chunk):
        far_copy(chunk).wait_send()

        @pl.when(chunk + WINDOW < CHUNKS)
        def _():
            send([chunk + WINDOW], [])

    def refill_near(chunk):
        near_copy(chunk).wait_send()

        @pl.when(chunk + WINDOW < CHUNKS)
        def _():
            send([], [chunk + WINDOW])

    def across(chunk, carry):
        refill_far(chunk)
        far_copy(chunk).wait_recv()
        pass_copy(chunk).start()
        factor = jnp.where(chunk == CHUNKS - 1, scale, 1.0)
        gather(0, got_far, pl.multiple_of(chunk * CHUNK, CHUNK), CHUNK, False, factor)
        refill_near(chunk)
        near_copy(chunk).wait_recv()
        pass_copy(chunk).wait()

        @pl.when(chunk < CHUNKS - 1)
        def _():
            gather(1, met, pl.multiple_of(2 * chunk * CHUNK, CHUNK), 2 * CHUNK)

        return carry

    lax.fori_loop(0, CHUNKS, across, 0)


def closing(scale_ref, shift_ref, own, met, grads, losses, loss_out, image_out, text_out, scaled, cost, sem):
    parity = lax.rem(lax.axis_index("rep"), 2)
    scale = scale_ref[0]
    shift = shift_ref[0]
    tiles = ROWS // TILE

    def store(source, output, tile, which):
        part = pl.ds(tile * TILE, TILE)
        return pltpu.make_async_copy(source.at[part], output.at[part], sem.at[which * tiles + tile])

    for side, output in enumerate((text_out, image_out)):

        @pl.when(parity == side)
        def _():
            for tile in range(tiles):
                store(grads.at[0], output, tile, 0).start()

    block = met[pl.ds(2 * (ROWS - CHUNK), 2 * CHUNK), :]
    for tile in range(tiles):
        part = pl.ds(tile * TILE, TILE)
        total, change = meet(own.at[1], block, scale, shift, tile)
        scaled[part, :] = (grads[1, part, :] + change) * scale

        for side, output in enumerate((image_out, text_out)):

            @pl.when(parity == side)
            def _():
                store(scaled, output, tile, 1).start()

        image_losses = jnp.where(parity == 0, losses[1, part, :] + total, losses[0, part, :])
        cost[part] = jnp.sum(image_losses.T, axis=0)
    loss_store = pltpu.make_async_copy(cost, loss_out, sem.at[2 * tiles])
    loss_store.start()
    for tile in range(tiles):
        store(grads.at[0], text_out, tile, 0).wait()
        store(scaled, image_out, tile, 1).wait()
    loss_store.wait()


def shards(picture_embeds, caption_embeds, sharpness_multiplier, offset_shift):
    smem = pl.BlockSpec(memory_space=pltpu.SMEM)
    vmem = pl.BlockSpec(memory_space=pltpu.VMEM)
    hbm = pl.BlockSpec(memory_space=pltpu.HBM)
    block = pltpu.VMEM((ROWS, WIDTH), jnp.bfloat16)
    chunk_sems = pltpu.SemaphoreType.DMA((CHUNKS,))
    kept = pl.pallas_call(
        kernel,
        out_shape=[
            pltpu.VMEM((2, ROWS, WIDTH), jnp.bfloat16),
            pltpu.VMEM((2 * ROWS, WIDTH), jnp.bfloat16),
            pltpu.VMEM((2, ROWS, WIDTH), jnp.float32),
            pltpu.VMEM((2, ROWS, 128), jnp.float32),
        ],
        in_specs=[smem, smem, hbm, hbm],
        out_specs=[vmem] * 4,
        scratch_shapes=[
            block, block,
            pltpu.SemaphoreType.DMA((2,)),
            chunk_sems, chunk_sems, chunk_sems, chunk_sems, chunk_sems, chunk_sems,
            pltpu.SemaphoreType.DMA((2,)),
        ],
        compiler_params=pltpu.CompilerParams(
            collective_id=0, has_side_effects=True, vmem_limit_bytes=40 * 2**20
        ),
        cost_estimate=pl.CostEstimate(
            flops=24 * ROWS * ROWS * WIDTH, bytes_accessed=12 * ROWS * WIDTH, transcendentals=18 * ROWS * ROWS
        ),
    )(
        sharpness_multiplier,
        offset_shift,
        pltpu.with_memory_space_constraint(caption_embeds, pltpu.HBM),
        pltpu.with_memory_space_constraint(picture_embeds, pltpu.HBM),
    )
    kept = [pltpu.with_memory_space_constraint(value, pltpu.VMEM) for value in kept]
    return pl.pallas_call(
        closing,
        out_shape=[
            jax.ShapeDtypeStruct((ROWS,), jnp.float32),
            jax.ShapeDtypeStruct((ROWS, WIDTH), jnp.float32),
            jax.ShapeDtypeStruct((ROWS, WIDTH), jnp.float32),
        ],
        in_specs=[smem, smem, vmem, vmem, vmem, vmem],
        out_specs=[hbm, hbm, hbm],
        scratch_shapes=[
            pltpu.VMEM((ROWS, WIDTH), jnp.float32),
            pltpu.VMEM((ROWS,), jnp.float32),
            pltpu.SemaphoreType.DMA((2 * ROWS // TILE + 1,)),
        ],
        compiler_params=pltpu.CompilerParams(vmem_limit_bytes=40 * 2**20),
        cost_estimate=pl.CostEstimate(
            flops=8 * CHUNK * ROWS * WIDTH, bytes_accessed=8 * ROWS * WIDTH, transcendentals=6 * CHUNK * ROWS
        ),
    )(sharpness_multiplier, offset_shift, *kept)


def solution(mesh):
    in_specs = (P(("dp", "rep"), None), P(("dp", "rep"), None), P(), P())
    out_specs = (P(("dp", "rep")), P(("dp", "rep"), None), P(("dp", "rep"), None))
    return jax.shard_map(shards, mesh=mesh, in_specs=in_specs, out_specs=out_specs, check_vma=False)
```

```python
import jax
import jax.numpy as jnp
from jax import lax
from jax.experimental import pallas as pl
from jax.experimental.pallas import tpu as pltpu
from jax.sharding import PartitionSpec as P

MESH = pl.DeviceIdType.MESH
N_REP = 4
DEVICES = 256
ROWS = 768
WIDTH = 1152
CHUNK = 128
CHUNKS = ROWS // CHUNK
TILE = 256
WINDOW = 2


def meet(near_or_far, block, scale, shift, tile, start=None):
    part = pl.ds(pl.multiple_of(jnp.int32(tile) * TILE, TILE), TILE)
    count = block.shape[0]
    logits = (
        lax.dot_general(
            near_or_far[part, :], block, (((1,), (1,)), ((), ())), preferred_element_type=jnp.float32
        )
        * scale
        + shift
    )
    decay = jnp.exp(-jnp.abs(logits))
    above = 1.0 + decay
    inverse = pl.reciprocal(above, approx=True)
    inverse = inverse * (2.0 - above * inverse)
    chance = jnp.where(logits >= 0, inverse, decay * inverse)
    log_above = jnp.log(above) + (decay - (above - 1.0)) * inverse
    if start is not None:
        row = lax.broadcasted_iota(jnp.int32, (TILE, count), 0) + tile * TILE
        column = lax.broadcasted_iota(jnp.int32, (TILE, count), 1) + start
        same = row == column
        chance = chance - jnp.where(same, 1.0, 0.0)
        logits = jnp.where(same, -logits, logits)
    cost = jnp.maximum(logits, 0.0) + log_above
    total = cost[:, : min(count, 128)]
    for piece in range(1, count // 128):
        total = total + cost[:, piece * 128 : (piece + 1) * 128]
    change = jnp.dot(chance.astype(jnp.bfloat16), block, preferred_element_type=jnp.float32)
    return total, change


def kernel(
    scale_ref, shift_ref, text_ref, image_ref,
    own, met, grads, losses,
    got_far, beside,
    load_sem, far_send, far_recv, near_send, near_recv, pass_send, pass_recv, beside_sem,
):
    dp, rep = lax.axis_index("dp"), lax.axis_index("rep")
    parity = lax.rem(rep, 2)
    me = dp * N_REP + rep

    def place(index):
        index = lax.rem(index + DEVICES, DEVICES)
        return (index // N_REP, lax.rem(index, N_REP))

    far_target = place(me - 2 + 4 * parity)
    near_target = place(me + 2 - 4 * parity)
    partner = (dp, rep + 1 - 2 * parity)

    loads = [
        pltpu.make_async_copy(text_ref, own.at[parity], load_sem.at[0]),
        pltpu.make_async_copy(image_ref, own.at[1 - parity], load_sem.at[1]),
    ]
    for load in loads:
        load.start()
    barrier = pltpu.get_barrier_semaphore()
    for target in (far_target, near_target, partner):
        pl.semaphore_signal(barrier, inc=1, device_id=target, device_id_type=MESH)

    scale = scale_ref[0]
    shift = shift_ref[0]

    def rows(chunk):
        return pl.ds(pl.multiple_of(chunk * CHUNK, CHUNK), CHUNK)

    def far_copy(chunk, source=image_ref):
        return pltpu.make_async_remote_copy(
            src_ref=source.at[rows(chunk)], dst_ref=got_far.at[rows(chunk)],
            send_sem=far_send.at[chunk], recv_sem=far_recv.at[chunk],
            device_id=far_target, device_id_type=MESH,
        )

    def near_copy(chunk, source=text_ref):
        return pltpu.make_async_remote_copy(
            src_ref=source.at[rows(chunk)], dst_ref=met.at[rows(2 * chunk + 1)],
            send_sem=near_send.at[chunk], recv_sem=near_recv.at[chunk],
            device_id=near_target, device_id_type=MESH,
        )

    def beside_copy(source=text_ref):
        return pltpu.make_async_remote_copy(
            src_ref=source, dst_ref=beside, send_sem=beside_sem.at[0], recv_sem=beside_sem.at[1],
            device_id=partner, device_id_type=MESH,
        )

    def pass_copy(chunk):
        return pltpu.make_async_remote_copy(
            src_ref=got_far.at[rows(chunk)], dst_ref=met.at[rows(2 * chunk)],
            send_sem=pass_send.at[chunk], recv_sem=pass_recv.at[chunk],
            device_id=partner, device_id_type=MESH,
        )

    def send(fars, nears, with_beside=False):
        for side, (far_source, near_source) in enumerate(((image_ref, text_ref), (text_ref, image_ref))):

            @pl.when(parity == side)
            def _():
                for step in range(max(len(fars), len(nears))):
                    if step < len(fars):
                        far_copy(fars[step], far_source).start()
                    if step < len(nears):
                        near_copy(nears[step], near_source).start()
                    if step == 0 and with_beside:
                        beside_copy(near_source).start()

    def gather(slot, other, start, count, diagonal=False, factor=None):
        block = other[pl.ds(start, count), :]

        def one(tile, carry):
            part = pl.ds(pl.multiple_of(tile * TILE, TILE), TILE)
            total, change = meet(own.at[slot], block, scale, shift, tile, start if diagonal else None)
            losses[slot, part, : total.shape[1]] += total
            if factor is None:
                grads[slot, part, :] += change
            else:
                grads[slot, part, :] = (grads[slot, part, :] + change) * factor
            return carry

        for tile in range(ROWS // TILE):
            one(tile, 0)

    pl.semaphore_wait(barrier, 3)
    send(range(WINDOW), [], True)
    grads[...] = jnp.zeros_like(grads)
    losses[...] = jnp.zeros_like(losses)
    for load in loads:
        load.wait()

    def local(step, carry):
        @pl.when(step == 1)
        def _():
            send([], range(WINDOW))

        slot = lax.rem(step, 2)
        gather(slot, own.at[1 - slot], pl.multiple_of(step // 2 * TILE, TILE), TILE, True)
        return carry

    lax.fori_loop(0, 2 * ROWS // TILE, local, 0)
    beside_copy().wait()

    def inside(step, carry):
        gather(0, beside, pl.multiple_of(step * TILE, TILE), 256)
        return carry

    lax.fori_loop(0, ROWS // TILE, inside, 0)

    def refill_far(chunk):
        far_copy(chunk).wait_send()

        @pl.when(chunk + WINDOW < CHUNKS)
        def _():
            send([chunk + WINDOW], [])

    def refill_near(chunk):
        near_copy(chunk).wait_send()

        @pl.when(chunk + WINDOW < CHUNKS)
        def _():
            send([], [chunk + WINDOW])

    def across(chunk, carry):
        refill_far(chunk)
        far_copy(chunk).wait_recv()
        pass_copy(chunk).start()
        factor = jnp.where(chunk == CHUNKS - 1, scale, 1.0)
        gather(0, got_far, pl.multiple_of(chunk * CHUNK, CHUNK), CHUNK, False, factor)
        refill_near(chunk)
        near_copy(chunk).wait_recv()
        pass_copy(chunk).wait()

        @pl.when(chunk < CHUNKS - 1)
        def _():
            gather(1, met, pl.multiple_of(2 * chunk * CHUNK, CHUNK), 2 * CHUNK)

        return carry

    lax.fori_loop(0, CHUNKS, across, 0)


def closing(scale_ref, shift_ref, own, met, grads, losses, loss_out, image_out, text_out, scaled, cost, sem):
    parity = lax.rem(lax.axis_index("rep"), 2)
    scale = scale_ref[0]
    shift = shift_ref[0]
    tiles = ROWS // TILE

    def store(source, output, tile, which):
        part = pl.ds(tile * TILE, TILE)
        return pltpu.make_async_copy(source.at[part], output.at[part], sem.at[which * tiles + tile])

    for side, output in enumerate((text_out, image_out)):

        @pl.when(parity == side)
        def _():
            for tile in range(tiles):
                store(grads.at[0], output, tile, 0).start()

    block = met[pl.ds(2 * (ROWS - CHUNK), 2 * CHUNK), :]
    for tile in range(tiles):
        part = pl.ds(tile * TILE, TILE)
        total, change = meet(own.at[1], block, scale, shift, tile)
        scaled[part, :] = (grads[1, part, :] + change) * scale

        for side, output in enumerate((image_out, text_out)):

            @pl.when(parity == side)
            def _():
                store(scaled, output, tile, 1).start()

        image_losses = jnp.where(parity == 0, losses[1, part, :] + total, losses[0, part, :])
        cost[part] = jnp.sum(image_losses.T, axis=0)
    loss_store = pltpu.make_async_copy(cost, loss_out, sem.at[2 * tiles])
    loss_store.start()
    for tile in range(tiles):
        store(grads.at[0], text_out, tile, 0).wait()
        store(scaled, image_out, tile, 1).wait()
    loss_store.wait()


def shards(picture_embeds, caption_embeds, sharpness_multiplier, offset_shift):
    smem = pl.BlockSpec(memory_space=pltpu.SMEM)
    vmem = pl.BlockSpec(memory_space=pltpu.VMEM)
    hbm = pl.BlockSpec(memory_space=pltpu.HBM)
    block = pltpu.VMEM((ROWS, WIDTH), jnp.bfloat16)
    chunk_sems = pltpu.SemaphoreType.DMA((CHUNKS,))
    kept = pl.pallas_call(
        kernel,
        out_shape=[
            pltpu.VMEM((2, ROWS, WIDTH), jnp.bfloat16),
            pltpu.VMEM((2 * ROWS, WIDTH), jnp.bfloat16),
            pltpu.VMEM((2, ROWS, WIDTH), jnp.float32),
            pltpu.VMEM((2, ROWS, 128), jnp.float32),
        ],
        in_specs=[smem, smem, hbm, hbm],
        out_specs=[vmem] * 4,
        scratch_shapes=[
            block, block,
            pltpu.SemaphoreType.DMA((2,)),
            chunk_sems, chunk_sems, chunk_sems, chunk_sems, chunk_sems, chunk_sems,
            pltpu.SemaphoreType.DMA((2,)),
        ],
        compiler_params=pltpu.CompilerParams(
            collective_id=0, has_side_effects=True, vmem_limit_bytes=40 * 2**20
        ),
        cost_estimate=pl.CostEstimate(
            flops=24 * ROWS * ROWS * WIDTH, bytes_accessed=12 * ROWS * WIDTH, transcendentals=18 * ROWS * ROWS
        ),
    )(
        sharpness_multiplier,
        offset_shift,
        pltpu.with_memory_space_constraint(caption_embeds, pltpu.HBM),
        pltpu.with_memory_space_constraint(picture_embeds, pltpu.HBM),
    )
    kept = [pltpu.with_memory_space_constraint(value, pltpu.VMEM) for value in kept]
    return pl.pallas_call(
        closing,
        out_shape=[
            jax.ShapeDtypeStruct((ROWS,), jnp.float32),
            jax.ShapeDtypeStruct((ROWS, WIDTH), jnp.float32),
            jax.ShapeDtypeStruct((ROWS, WIDTH), jnp.float32),
        ],
        in_specs=[smem, smem, vmem, vmem, vmem, vmem],
        out_specs=[hbm, hbm, hbm],
        scratch_shapes=[
            pltpu.VMEM((ROWS, WIDTH), jnp.float32),
            pltpu.VMEM((ROWS,), jnp.float32),
            pltpu.SemaphoreType.DMA((2 * ROWS // TILE + 1,)),
        ],
        compiler_params=pltpu.CompilerParams(vmem_limit_bytes=40 * 2**20),
        cost_estimate=pl.CostEstimate(
            flops=8 * CHUNK * ROWS * WIDTH, bytes_accessed=8 * ROWS * WIDTH, transcendentals=6 * CHUNK * ROWS
        ),
    )(sharpness_multiplier, offset_shift, *kept)


def solution(mesh):
    in_specs = (P(("dp", "rep"), None), P(("dp", "rep"), None), P(), P())
    out_specs = (P(("dp", "rep")), P(("dp", "rep"), None), P(("dp", "rep"), None))
    return jax.shard_map(shards, mesh=mesh, in_specs=in_specs, out_specs=out_specs, check_vma=False)
```
